256 devices in a mesh: row: 32 (over z_hi, x, core), col: 8 (over z_lo, y).
Axes of the slice: x: 4, y: 4, z: 8 (z_hi: 4, z_lo: 2; z = z_hi * 2 + z_lo), core: 2. Of those that a mesh axis runs over, the one named last changes fastest.
Arguments:
- activations: bfloat16 [4096, 8192], P(None, 'row'), may hold values from -6 to 6
- stored_head_inputs: bfloat16 [4096, 8192], P('row', 'col'), may hold values from -10 to 10
- joined_weight: bfloat16 [8192, 8192], P('row', 'col'), may hold values from -0.0625 to 0.0625
- output_weight: bfloat16 [6144, 8192], P('col', 'row'), may hold values from -0.078125 to 0.078125
- upstream: bfloat16 [4096, 8192], P(None, 'row'), may hold values from -6 to 6
Outputs:
- grad_activations: bfloat16 [4096, 8192], P(None, 'row')
- grad_joined: bfloat16 [8192, 8192], P('row', 'col')
- grad_output: bfloat16 [6144, 8192], P('col', 'row')
The draws below stay inside these ranges and needn't reach their ends.
All inputs are finite; a program needn't handle non-finite values.
Results may differ from the reference program's by a relative error of at most 0.0071.
Values may be sent and summed in bfloat16 or wider, within the bound.
A program may use at most 128 MiB of HBM per device.

```python
import jax
import jax.numpy as jnp
from jax import lax

D = 8192
HQ = 48
KV_HEAD_COUNT = 8
HEAD_SIZE = 128
QUERIES_PER_KV = 6
GROUP_WIDTH = 1024
QKV = 8192
HA = 6144
TOKEN_COUNT = 4096


def draw_stored_head_inputs(key, part):
    key = jax.random.fold_in(key, 11)
    random_base_key = jax.random.fold_in(key, 0)
    fresh_result = jnp.clip(jax.random.normal(random_base_key, (TOKEN_COUNT, KV_HEAD_COUNT, GROUP_WIDTH), jnp.float32), -4.0, 4.0)
    return fresh_result.reshape(TOKEN_COUNT, KV_HEAD_COUNT * GROUP_WIDTH).astype(jnp.bfloat16)


def strengthened(drawn, stream_key, source, target, blocks, factor):
    def block_of(axis_at):
        return (jnp.arange(drawn.shape[axis_at]) // (drawn.shape[axis_at] // blocks)).reshape((-1,) + (1,) * (drawn.ndim - 1 - axis_at))

    first = jax.random.permutation(stream_key, blocks)[block_of(target)]
    other_side = (block_of(target) + blocks // 2) % blocks
    return jnp.where((block_of(source) == first) | (block_of(source) == other_side), factor * drawn, drawn)


def block_levels(stream_key, dims, cuts, least, high):
    loudness = 1.0
    for dim, blocks in cuts:
        steps = jax.random.uniform(jax.random.fold_in(jax.random.fold_in(stream_key, 6), dim), (blocks,), jnp.float32, least / len(cuts), high / len(cuts))
        loudness = loudness * jnp.repeat(jnp.exp(steps), dims[dim] // blocks).reshape((-1,) + (1,) * (len(dims) - 1 - dim))
    return loudness


def noise(key, shape, scale, reach, cuts=(), held_as=jnp.bfloat16):
    array = scale * jax.random.normal(key, shape, jnp.float32)
    if cuts:
        array = array * block_levels(key, shape, cuts, -0.22, 0.18)
    return jnp.clip(array, -reach, reach).astype(held_as)


def gaussian_with(rng, extent, spread, most, pieces, heavy, kind=jnp.bfloat16):
    array = spread * jax.random.normal(rng, extent, jnp.float32)
    if pieces:
        array = array * block_levels(rng, extent, pieces, -0.22, 0.18)
    return jnp.clip(strengthened(array, jax.random.fold_in(rng, 3), *heavy), -most, most).astype(kind)


def setup_inputs(seed: int = 0) -> dict:
    streams_of = jax.random.split(jax.random.key(seed), 6)
    return {
        "activations": noise(streams_of[0], (TOKEN_COUNT, D), 1.0, 6.0, ((1, 32),)),
        "stored_head_inputs": draw_stored_head_inputs(jax.random.fold_in(streams_of[5], 71), 0),
        "joined_weight": noise(streams_of[2], (D, QKV), D ** -0.5, 0.0625, ((0, 32), (1, 8))),
        "output_weight": noise(streams_of[3], (HA, D), HA ** -0.5, 0.078125, ((0, 8), (1, 32))),
        "upstream": gaussian_with(streams_of[4], (TOKEN_COUNT, D), 0.5, 6.0, ((1, 32),), (1, 0, 32, 2.75)),
    }


def one_head(query, dgrad, key_rows, value_rows):
    positions = jnp.arange(query.shape[0], dtype=jnp.int32)
    allowed = positions[None, :] <= positions[:, None]
    attention_score_scale = HEAD_SIZE ** -0.5
    scores = jnp.dot(query, key_rows.T, preferred_element_type=jnp.float32) * attention_score_scale
    masked = jnp.where(allowed, scores, -1e30)
    highest = jnp.max(masked, axis=1, keepdims=True)
    expon = jnp.where(allowed, jnp.exp(masked - highest), 0.0)
    weights_f = expon / jnp.sum(expon, axis=1, keepdims=True)
    weights_b = weights_f.astype(jnp.bfloat16)
    attn_f = jnp.dot(weights_b, value_rows, preferred_element_type=jnp.float32)
    delta_row = jnp.sum(dgrad.astype(jnp.float32) * attn_f, axis=1, keepdims=True)
    dprob = jnp.dot(dgrad, value_rows.T, preferred_element_type=jnp.float32)
    dscore = (weights_f * (dprob - delta_row)).astype(jnp.bfloat16)
    query_gradient = jnp.dot(dscore, key_rows, preferred_element_type=jnp.float32) * attention_score_scale
    key_gradient = jnp.dot(dscore.T, query, preferred_element_type=jnp.float32)
    value_gradient = jnp.dot(weights_b.T, dgrad, preferred_element_type=jnp.float32)
    return attn_f.astype(jnp.bfloat16), query_gradient, key_gradient, value_gradient


def reference(activations, stored_head_inputs, joined_weight, output_weight, upstream):
    dout_f = lax.dot_general(upstream, output_weight, (((1,), (1,)), ((), ())), preferred_element_type=jnp.float32)
    grad_attn = dout_f.astype(jnp.bfloat16)
    grouped_heads = stored_head_inputs.reshape(TOKEN_COUNT, KV_HEAD_COUNT, GROUP_WIDTH)
    queries = grouped_heads[:, :, :QUERIES_PER_KV * HEAD_SIZE].reshape(TOKEN_COUNT, HQ, HEAD_SIZE).transpose(1, 0, 2)
    key_heads = grouped_heads[:, :, QUERIES_PER_KV * HEAD_SIZE:(QUERIES_PER_KV + 1) * HEAD_SIZE].transpose(1, 0, 2)
    value_heads = grouped_heads[:, :, (QUERIES_PER_KV + 1) * HEAD_SIZE:].transpose(1, 0, 2)
    dout_heads = grad_attn.reshape(TOKEN_COUNT, HQ, HEAD_SIZE).transpose(1, 0, 2)

    def per_head(element):
        query, dgrad, head = element
        group_index = head // QUERIES_PER_KV
        key_rows = lax.dynamic_index_in_dim(key_heads, group_index, 0, keepdims=False)
        value_rows = lax.dynamic_index_in_dim(value_heads, group_index, 0, keepdims=False)
        return one_head(query, dgrad, key_rows, value_rows)

    attn, query_gradient, key_gradient, value_gradient = lax.map(per_head, (queries, dout_heads, jnp.arange(HQ, dtype=jnp.int32)))
    attention_score_scale = HEAD_SIZE ** -0.5
    key_gradient = (jnp.sum(key_gradient.reshape(KV_HEAD_COUNT, QUERIES_PER_KV, TOKEN_COUNT, HEAD_SIZE), axis=1) * attention_score_scale).astype(jnp.bfloat16).transpose(1, 0, 2)
    value_gradient = jnp.sum(value_gradient.reshape(KV_HEAD_COUNT, QUERIES_PER_KV, TOKEN_COUNT, HEAD_SIZE), axis=1).astype(jnp.bfloat16).transpose(1, 0, 2)
    query_gradient = query_gradient.astype(jnp.bfloat16).transpose(1, 0, 2).reshape(TOKEN_COUNT, KV_HEAD_COUNT, QUERIES_PER_KV * HEAD_SIZE)
    grad_heads = jnp.concatenate([query_gradient, key_gradient, value_gradient], axis=2).reshape(TOKEN_COUNT, QKV)
    attn_rows = attn.transpose(1, 0, 2).reshape(TOKEN_COUNT, HA)
    grad_output = lax.dot_general(attn_rows, upstream, (((0,), (0,)), ((), ())), preferred_element_type=jnp.float32).astype(jnp.bfloat16)
    grad_joined = lax.dot_general(activations, grad_heads, (((0,), (0,)), ((), ())), preferred_element_type=jnp.float32).astype(jnp.bfloat16)
    grad_activations = lax.dot_general(grad_heads, joined_weight, (((1,), (1,)), ((), ())), preferred_element_type=jnp.float32).astype(jnp.bfloat16)
    return grad_activations, grad_joined, grad_output
```

```python
import jax
import jax.numpy as jnp
from jax import lax
from jax.experimental import pallas as pl
from jax.experimental.pallas import tpu as pltpu
from jax.sharding import PartitionSpec as P

HEAD_SIZE = 128
QUERIES_PER_KV = 6
GROUP_WIDTH = 1024
KEY_TILE = 512
LOG2E = 1.4426950408889634
MESH = pl.DeviceIdType.MESH
NT = (((1,), (1,)), ((), ()))


class Place:
    def __init__(self):
        self.row, self.col = lax.axis_index("row"), lax.axis_index("col")
        self.z, self.x, self.core = self.row // 8, (self.row // 2) % 4, self.row % 2
        self.low, self.y = self.col // 4, self.col % 4
        self.right, self.left, self.far = (self.x + 1) % 4, (self.x + 3) % 4, (self.x + 2) % 4
        self.y_right, self.y_left = (self.y + 1) % 4, (self.y + 3) % 4
        self.y_far = (self.y + 2) % 4

    def to_x(self, x):
        return (self.z * 8 + x * 2 + self.core, self.col)

    def to_z(self, z):
        return (z * 8 + self.x * 2 + self.core, self.col)

    def sibling(self):
        return (self.z * 8 + self.x * 2 + 1 - self.core, self.col)

    def to_y(self, y):
        return (self.row, self.low * 4 + y)

    def to_low(self):
        return (self.row, (1 - self.low) * 4 + self.y)

    def row_peers(self):
        return [
            self.sibling(),
            self.to_x(self.right),
            self.to_x(self.left),
            *[self.to_z((self.z + step) % 4) for step in (1, 2, 3)],
        ]

    def col_peers(self):
        return [self.to_y(self.y_right), self.to_y(self.y_left), self.to_low()]


def greet(peers):
    barrier = pltpu.get_barrier_semaphore()
    for peer in peers:
        pl.semaphore_signal(barrier, inc=1, device_id=peer, device_id_type=MESH)
    pl.semaphore_wait(barrier, len(peers))


class Copy:
    def __init__(self, pool, source, target, device, arrival):
        send, recv = pool.next_pair()
        pool.started.append(self)
        self.out = pltpu.make_async_remote_copy(
            src_ref=source, dst_ref=target, send_sem=send, recv_sem=recv,
            device_id=device, device_id_type=MESH,
        )
        self.into = pltpu.make_async_remote_copy(
            src_ref=arrival, dst_ref=arrival, send_sem=send, recv_sem=recv,
            device_id=device, device_id_type=MESH,
        )
        self.out.start()

    def arrived(self):
        self.into.wait_recv()


class Pool:
    def __init__(self, send, recv):
        self.send, self.recv, self.used, self.started = send, recv, 0, []

    def next_pair(self):
        self.used += 1
        return self.send.at[self.used - 1], self.recv.at[self.used - 1]

    def drain(self):
        for copy in self.started:
            copy.out.wait_send()


class RowGather:
    def __init__(self, place, pool, buffer):
        self.place, self.pool, self.buffer = place, pool, buffer
        self.core_copies = {}

    def z_start(self, block):
        p, own = self.place, None
        own = self.buffer.at[p.z, p.x, p.core]
        self.z_copies = [
            Copy(
                self.pool, block, own, p.to_z((p.z + step) % 4),
                self.buffer.at[(p.z + 4 - step) % 4, p.x, p.core],
            )
            for step in (1, 2, 3)
        ]

    def x_start(self):
        p, b = self.place, self.buffer
        for copy in self.z_copies:
            copy.arrived()
        column = b.at[:, p.x, p.core]
        self.from_left = Copy(self.pool, column, column, p.to_x(p.right), b.at[:, p.left, p.core])
        self.from_right = Copy(self.pool, column, column, p.to_x(p.left), b.at[:, p.right, p.core])
        self.core_start("own", p.x)

    def core_start(self, name, x):
        p, b = self.place, self.buffer
        column = b.at[:, x, p.core]
        self.core_copies[name] = Copy(
            self.pool, column, column, p.sibling(), b.at[:, x, 1 - p.core]
        )

    def forward(self):
        p, b = self.place, self.buffer
        self.from_left.arrived()
        low = b.at[0:2, p.left, p.core]
        self.far_low = Copy(self.pool, low, low, p.to_x(p.right), b.at[0:2, p.far, p.core])
        self.from_right.arrived()
        high = b.at[2:4, p.right, p.core]
        self.far_high = Copy(self.pool, high, high, p.to_x(p.left), b.at[2:4, p.far, p.core])
        self.core_start("left", p.left)
        self.core_start("right", p.right)

    def far_core(self):
        self.far_low.arrived()
        self.far_high.arrived()
        self.core_start("far", self.place.far)

    def wait_core(self, name):
        self.core_copies[name].arrived()


class RowScatter:
    def __init__(self, place, pool, parts, halves, sums, z_out, z_in):
        self.place, self.pool, self.parts = place, pool, parts
        self.halves, self.sums, self.z_out, self.z_in = halves, sums, z_out, z_in

    def far_start(self):
        p, q = self.place, self.parts
        self.half_left = Copy(
            self.pool, q.at[p.far, 0:2], self.halves.at[0], p.to_x(p.right), self.halves.at[0]
        )
        self.half_right = Copy(
            self.pool, q.at[p.far, 2:4], self.halves.at[1], p.to_x(p.left), self.halves.at[1]
        )

    def near_start(self):
        p, q, s = self.place, self.parts, self.sums
        self.direct = [
            Copy(self.pool, q.at[p.right, 2:4], s.at[0, 2:4], p.to_x(p.right), s.at[0, 2:4]),
            Copy(self.pool, q.at[p.left, 0:2], s.at[1, 0:2], p.to_x(p.left), s.at[1, 0:2]),
        ]

    def relay(self):
        p, q, s = self.place, self.parts, self.sums
        self.half_left.arrived()
        for z in (0, 1):
            q[p.right, z] = (
                q[p.right, z].astype(jnp.float32) + self.halves[0, z].astype(jnp.float32)
            ).astype(jnp.bfloat16)
        self.direct.append(
            Copy(self.pool, q.at[p.right, 0:2], s.at[0, 0:2], p.to_x(p.right), s.at[0, 0:2])
        )
        self.half_right.arrived()
        for z in (0, 1):
            q[p.left, z + 2] = (
                q[p.left, z + 2].astype(jnp.float32) + self.halves[1, z].astype(jnp.float32)
            ).astype(jnp.bfloat16)
        self.direct.append(
            Copy(self.pool, q.at[p.left, 2:4], s.at[1, 2:4], p.to_x(p.left), s.at[1, 2:4])
        )

    def z_start(self):
        p = self.place
        for copy in self.direct:
            copy.arrived()

        def total(z):
            return (
                self.parts[p.x, z].astype(jnp.float32)
                + self.sums[0, z].astype(jnp.float32)
                + self.sums[1, z].astype(jnp.float32)
            )

        self.z_copies = []
        for step in (1, 2, 3):
            z = (p.z + step) % 4
            self.z_out[step - 1] = total(z).astype(jnp.bfloat16)
            self.z_copies.append(
                Copy(
                    self.pool, self.z_out.at[step - 1], self.z_in.at[step - 1], p.to_z(z),
                    self.z_in.at[step - 1],
                )
            )
        self.own = total(p.z)

    def finish(self):
        for copy in self.z_copies:
            copy.arrived()
        return (
            self.own
            + self.z_in[0].astype(jnp.float32)
            + self.z_in[1].astype(jnp.float32)
            + self.z_in[2].astype(jnp.float32)
        )


def scatter_kernel(
    upstream, weight, kv_own, grad_ref, kv_all, other_up, other_weight, parts, halves, sums,
    z_out, z_in, send, recv,
):
    p, pool = Place(), Pool(send, recv)
    chunks = parts.shape[0]
    width = parts.shape[-1]
    greet(p.row_peers())
    other = 1 - p.core
    weight_copy = Copy(pool, weight, other_weight, p.sibling(), other_weight)
    order = (p.far, p.right, p.left, p.x)
    up_copies = [
        Copy(pool, upstream.at[:, x, other], other_up.at[:, x], p.sibling(), other_up.at[:, x])
        for x in order
    ]
    gather = RowGather(p, pool, kv_all)
    gather.z_start(kv_own)
    kv_all[p.z, p.x, p.core] = kv_own[...]
    scatters = [
        RowScatter(p, pool, parts.at[j], halves.at[j], sums.at[j], z_out.at[j], z_in.at[j])
        for j in range(chunks)
    ]

    def multiply(chunk, x):
        cols = pl.ds(chunk * width, width)
        for z in range(4):
            parts[chunk, x, z] = (
                lax.dot_general(
                    upstream[z, x, p.core], weight[cols, :], NT,
                    preferred_element_type=jnp.float32,
                )
                + lax.dot_general(
                    other_up[z, x], other_weight[cols, :], NT,
                    preferred_element_type=jnp.float32,
                )
            ).astype(jnp.bfloat16)

    weight_copy.arrived()
    for j in range(chunks):
        for index, x in enumerate(order):
            if j == 0:
                up_copies[index].arrived()
            multiply(j, x)
            if index == 0:
                scatters[j].far_start()
            if index == 2:
                scatters[j].near_start()
        if j == 0:
            gather.x_start()
    scatters[0].relay()
    gather.forward()
    scatters[1].relay()
    scatters[2].relay()
    scatters[0].z_start()
    gather.far_core()
    scatters[1].z_start()
    scatters[2].z_start()
    for j in range(chunks):
        grad_ref[:, pl.ds(j * width, width)] = scatters[j].finish().astype(jnp.bfloat16)
    for name in ("own", "left", "right", "far"):
        gather.wait_core(name)
    pool.drain()


def scatter_and_gather(upstream, weight, kv_own):
    tok_rows = kv_own.shape[0]
    features = upstream.shape[1]
    heads = weight.shape[0]
    chunks, width = 3, heads // 3
    vmem = pl.BlockSpec(memory_space=pltpu.VMEM)
    bf16 = jnp.bfloat16
    copies = 1 + 4 + 11 + 9 * chunks
    grad, kv_all = pl.pallas_call(
        scatter_kernel,
        out_shape=(
            jax.ShapeDtypeStruct((tok_rows, heads), bf16),
            jax.ShapeDtypeStruct((4, 4, 2, *kv_own.shape), bf16),
        ),
        in_specs=[vmem] * 3,
        out_specs=[vmem] * 2,
        scratch_shapes=[
            pltpu.VMEM((4, 4, tok_rows, features), bf16),
            pltpu.VMEM(weight.shape, bf16),
            pltpu.VMEM((chunks, 4, 4, tok_rows, width), bf16),
            pltpu.VMEM((chunks, 2, 2, tok_rows, width), bf16),
            pltpu.VMEM((chunks, 2, 4, tok_rows, width), bf16),
            pltpu.VMEM((chunks, 3, tok_rows, width), bf16),
            pltpu.VMEM((chunks, 3, tok_rows, width), bf16),
            pltpu.SemaphoreType.DMA((copies,)),
            pltpu.SemaphoreType.DMA((copies,)),
        ],
        compiler_params=pltpu.CompilerParams(
            collective_id=1, has_side_effects=True, vmem_limit_bytes=48 * 2**20
        ),
        name="grad_scatter",
    )(upstream.reshape(4, 4, 2, tok_rows, features), weight, kv_own)
    return grad, kv_all.reshape(-1, kv_own.shape[1])


def attention_kernel(
    stored_ref, kv_ref, grad_ref, attn_ref, dquery_ref, dkv_ref, score_ref, k_t, v_t, total_ref
):
    tok_rows = stored_ref.shape[0]
    tile = KEY_TILE
    first_token = lax.axis_index("row") * tok_rows
    tiles = (first_token + tok_rows + tile - 1) // tile
    pair_cols = 2 * tok_rows
    base2 = HEAD_SIZE ** (-0.5) * LOG2E

    def rows_of(index):
        return pl.ds(pl.multiple_of(index * tile, tile), tile)

    def prepare(index, carry):
        rows = rows_of(index)
        k_t[:, rows] = kv_ref[rows, :HEAD_SIZE].T
        v_t[:, rows] = kv_ref[rows, HEAD_SIZE:].T
        total_ref[rows, :] = jnp.zeros((tile, 2 * HEAD_SIZE), jnp.float32)
        return carry

    lax.fori_loop(0, kv_ref.shape[0] // tile, prepare, 0)

    def two_heads(ref, pair):
        start = pl.multiple_of(pair * 2 * HEAD_SIZE, 2 * HEAD_SIZE)
        both = ref[:, pl.ds(start, 2 * HEAD_SIZE)]
        return jnp.concatenate([both[:, :HEAD_SIZE], both[:, HEAD_SIZE:]], axis=0)

    def put_heads(ref, pair, stacked):
        start = pl.multiple_of(pair * 2 * HEAD_SIZE, 2 * HEAD_SIZE)
        ref[:, pl.ds(start, 2 * HEAD_SIZE)] = jnp.concatenate(
            [stacked[:tok_rows], stacked[tok_rows:]], axis=1
        )

    def one_pair(pair, carry):
        query = two_heads(stored_ref, pair)
        grad = two_heads(grad_ref, pair)
        query_t = query.T
        grad_t = grad.T

        def scores(index):
            return jnp.dot(
                kv_ref[rows_of(index), :HEAD_SIZE], query_t, preferred_element_type=jnp.float32
            )

        def fold(highest, block):
            return jnp.maximum(highest, jnp.max(block.reshape(tile // 8, 8, pair_cols), axis=0))

        def pass_scores(index, highest):
            block = scores(index)
            score_ref[rows_of(index), :] = block
            return fold(highest, block)

        highest = lax.fori_loop(
            0, tiles - 1, pass_scores, jnp.full((8, pair_cols), -3e38, jnp.float32)
        )
        last = tiles - 1
        key_pos = last * tile + lax.broadcasted_iota(jnp.int32, (tile, pair_cols), 0)
        token_pos = first_token + lax.broadcasted_iota(jnp.int32, (tile, pair_cols), 1) % tok_rows
        block = jnp.where(key_pos <= token_pos, scores(last), -1e30)
        score_ref[rows_of(last), :] = block
        highest = jnp.max(fold(highest, block), axis=0, keepdims=True) * base2

        def pass_exp(index, carry):
            total_exp, out_t = carry
            rows = rows_of(index)
            expon = jnp.exp2(score_ref[rows, :] * base2 - highest)
            score_ref[rows, :] = expon
            total_exp = total_exp + jnp.sum(expon.reshape(tile // 8, 8, pair_cols), axis=0)
            out_t = out_t + jnp.dot(
                v_t[:, rows], expon.astype(jnp.bfloat16), preferred_element_type=jnp.float32
            )
            return (total_exp, out_t)

        total_exp, out_t = lax.fori_loop(
            0,
            tiles,
            pass_exp,
            (
                jnp.zeros((8, pair_cols), jnp.float32),
                jnp.zeros((HEAD_SIZE, pair_cols), jnp.float32),
            ),
        )
        inverse = 1.0 / jnp.sum(total_exp, axis=0, keepdims=True)
        out_t = out_t * inverse
        delta = jnp.sum(out_t * grad_t.astype(jnp.float32), axis=0, keepdims=True)
        put_heads(attn_ref, pair, out_t.T.astype(jnp.bfloat16))

        def pass_grad(index, dquery_t):
            rows = rows_of(index)
            probs = score_ref[rows, :] * inverse
            dprob = jnp.dot(kv_ref[rows, HEAD_SIZE:], grad_t, preferred_element_type=jnp.float32)
            dscore = (probs * (dprob - delta)).astype(jnp.bfloat16)
            total_ref[rows, :HEAD_SIZE] += jnp.dot(
                dscore, query, preferred_element_type=jnp.float32
            )
            total_ref[rows, HEAD_SIZE:] += jnp.dot(
                probs.astype(jnp.bfloat16), grad, preferred_element_type=jnp.float32
            )
            return dquery_t + jnp.dot(k_t[:, rows], dscore, preferred_element_type=jnp.float32)

        dquery_t = lax.fori_loop(
            0, tiles, pass_grad, jnp.zeros((HEAD_SIZE, pair_cols), jnp.float32)
        )
        put_heads(
            dquery_ref, pair, (dquery_t * HEAD_SIZE ** (-0.5)).T.astype(jnp.bfloat16)
        )
        return carry

    lax.fori_loop(0, QUERIES_PER_KV // 2, one_pair, 0)

    def finish(index, carry):
        rows = rows_of(index)
        dkv_ref[rows, :HEAD_SIZE] = (total_ref[rows, :HEAD_SIZE] * HEAD_SIZE ** (-0.5)).astype(
            dkv_ref.dtype
        )
        dkv_ref[rows, HEAD_SIZE:] = total_ref[rows, HEAD_SIZE:].astype(dkv_ref.dtype)
        return carry

    lax.fori_loop(0, kv_ref.shape[0] // tile, finish, 0)


def attention(stored, kv, grad_attn, dkv_type):
    tok_rows, all_tokens = stored.shape[0], kv.shape[0]
    heads = QUERIES_PER_KV * HEAD_SIZE
    vmem = pl.BlockSpec(memory_space=pltpu.VMEM)
    pair_cols = 2 * tok_rows
    return pl.pallas_call(
        attention_kernel,
        out_shape=(
            jax.ShapeDtypeStruct((tok_rows, heads), jnp.bfloat16),
            jax.ShapeDtypeStruct((tok_rows, heads), jnp.bfloat16),
            jax.ShapeDtypeStruct((all_tokens, 2 * HEAD_SIZE), dkv_type),
        ),
        in_specs=[vmem] * 3,
        out_specs=[vmem] * 3,
        scratch_shapes=[
            pltpu.VMEM((all_tokens, pair_cols), jnp.float32),
            pltpu.VMEM((HEAD_SIZE, all_tokens), jnp.bfloat16),
            pltpu.VMEM((HEAD_SIZE, all_tokens), jnp.bfloat16),
            pltpu.VMEM((all_tokens, 2 * HEAD_SIZE), jnp.float32),
        ],
        compiler_params=pltpu.CompilerParams(vmem_limit_bytes=48 * 2**20),
        name="attention",
    )(stored, kv, grad_attn)


def local(activations, stored, joined_weight, output_weight, upstream):
    heads = QUERIES_PER_KV * HEAD_SIZE
    grad_attn, kv = scatter_and_gather(upstream, output_weight, stored[:, heads:])
    attn_local, dquery_local, dkv_part = attention(stored, kv, grad_attn, jnp.float32)
    dkv_all = lax.psum(dkv_part, "row").astype(jnp.bfloat16)
    attn_all = lax.all_gather(attn_local, "row", axis=0, tiled=True)
    dquery_all = lax.all_gather(dquery_local, "row", axis=0, tiled=True)
    grad_heads = jnp.concatenate([dquery_all, dkv_all], axis=1)
    grad_output = lax.dot_general(
        attn_all, upstream, (((0,), (0,)), ((), ())), preferred_element_type=jnp.float32
    ).astype(jnp.bfloat16)
    grad_joined = lax.dot_general(
        activations, grad_heads, (((0,), (0,)), ((), ())), preferred_element_type=jnp.float32
    ).astype(jnp.bfloat16)
    partial_input = lax.dot_general(
        grad_heads, joined_weight, (((1,), (1,)), ((), ())), preferred_element_type=jnp.float32
    )
    grad_activations = lax.psum(partial_input, "col").astype(jnp.bfloat16)
    return (grad_activations, grad_joined, grad_output)


def solution(mesh):
    return jax.shard_map(
        local,
        mesh=mesh,
        in_specs=(
            P(None, "row"),
            P("row", "col"),
            P("row", "col"),
            P("col", "row"),
            P(None, "row"),
        ),
        out_specs=(P(None, "row"), P("row", "col"), P("col", "row")),
        check_vma=False,
    )
```

```python
import jax
import jax.numpy as jnp
from jax import lax
from jax.experimental import pallas as pl
from jax.experimental.pallas import tpu as pltpu
from jax.sharding import PartitionSpec as P

HEAD_SIZE = 128
QUERIES_PER_KV = 6
GROUP_WIDTH = 1024
KEY_TILE = 512
LOG2E = 1.4426950408889634
MESH = pl.DeviceIdType.MESH
NT = (((1,), (1,)), ((), ()))


class Place:
    def __init__(self):
        self.row, self.col = lax.axis_index("row"), lax.axis_index("col")
        self.z, self.x, self.core = self.row // 8, (self.row // 2) % 4, self.row % 2
        self.low, self.y = self.col // 4, self.col % 4
        self.right, self.left, self.far = (self.x + 1) % 4, (self.x + 3) % 4, (self.x + 2) % 4
        self.y_right, self.y_left = (self.y + 1) % 4, (self.y + 3) % 4
        self.y_far = (self.y + 2) % 4

    def to_x(self, x):
        return (self.z * 8 + x * 2 + self.core, self.col)

    def to_z(self, z):
        return (z * 8 + self.x * 2 + self.core, self.col)

    def sibling(self):
        return (self.z * 8 + self.x * 2 + 1 - self.core, self.col)

    def to_y(self, y):
        return (self.row, self.low * 4 + y)

    def to_low(self):
        return (self.row, (1 - self.low) * 4 + self.y)

    def row_peers(self):
        return [
            self.sibling(),
            self.to_x(self.right),
            self.to_x(self.left),
            *[self.to_z((self.z + step) % 4) for step in (1, 2, 3)],
        ]

    def col_peers(self):
        return [self.to_y(self.y_right), self.to_y(self.y_left), self.to_low()]


def greet(peers):
    barrier = pltpu.get_barrier_semaphore()
    for peer in peers:
        pl.semaphore_signal(barrier, inc=1, device_id=peer, device_id_type=MESH)
    pl.semaphore_wait(barrier, len(peers))


class Copy:
    def __init__(self, pool, source, target, device, arrival):
        send, recv = pool.next_pair()
        pool.started.append(self)
        self.out = pltpu.make_async_remote_copy(
            src_ref=source, dst_ref=target, send_sem=send, recv_sem=recv,
            device_id=device, device_id_type=MESH,
        )
        self.into = pltpu.make_async_remote_copy(
            src_ref=arrival, dst_ref=arrival, send_sem=send, recv_sem=recv,
            device_id=device, device_id_type=MESH,
        )
        self.out.start()

    def arrived(self):
        self.into.wait_recv()


class Pool:
    def __init__(self, send, recv):
        self.send, self.recv, self.used, self.started = send, recv, 0, []

    def next_pair(self):
        self.used += 1
        return self.send.at[self.used - 1], self.recv.at[self.used - 1]

    def drain(self):
        for copy in self.started:
            copy.out.wait_send()


class RowGather:
    def __init__(self, place, pool, buffer):
        self.place, self.pool, self.buffer = place, pool, buffer
        self.core_copies = {}

    def z_start(self, block):
        p, own = self.place, None
        own = self.buffer.at[p.z, p.x, p.core]
        self.z_copies = [
            Copy(
                self.pool, block, own, p.to_z((p.z + step) % 4),
                self.buffer.at[(p.z + 4 - step) % 4, p.x, p.core],
            )
            for step in (1, 2, 3)
        ]

    def x_start(self):
        p, b = self.place, self.buffer
        for copy in self.z_copies:
            copy.arrived()
        column = b.at[:, p.x, p.core]
        self.from_left = Copy(self.pool, column, column, p.to_x(p.right), b.at[:, p.left, p.core])
        self.from_right = Copy(self.pool, column, column, p.to_x(p.left), b.at[:, p.right, p.core])
        self.core_start("own", p.x)

    def core_start(self, name, x):
        p, b = self.place, self.buffer
        column = b.at[:, x, p.core]
        self.core_copies[name] = Copy(
            self.pool, column, column, p.sibling(), b.at[:, x, 1 - p.core]
        )

    def forward(self):
        p, b = self.place, self.buffer
        self.from_left.arrived()
        low = b.at[0:2, p.left, p.core]
        self.far_low = Copy(self.pool, low, low, p.to_x(p.right), b.at[0:2, p.far, p.core])
        self.from_right.arrived()
        high = b.at[2:4, p.right, p.core]
        self.far_high = Copy(self.pool, high, high, p.to_x(p.left), b.at[2:4, p.far, p.core])
        self.core_start("left", p.left)
        self.core_start("right", p.right)

    def far_core(self):
        self.far_low.arrived()
        self.far_high.arrived()
        self.core_start("far", self.place.far)

    def wait_core(self, name):
        self.core_copies[name].arrived()


class RowScatter:
    def __init__(self, place, pool, parts, halves, sums, z_out, z_in):
        self.place, self.pool, self.parts = place, pool, parts
        self.halves, self.sums, self.z_out, self.z_in = halves, sums, z_out, z_in

    def far_start(self):
        p, q = self.place, self.parts
        self.half_left = Copy(
            self.pool, q.at[p.far, 0:2], self.halves.at[0], p.to_x(p.right), self.halves.at[0]
        )
        self.half_right = Copy(
            self.pool, q.at[p.far, 2:4], self.halves.at[1], p.to_x(p.left), self.halves.at[1]
        )

    def near_start(self):
        p, q, s = self.place, self.parts, self.sums
        self.direct = [
            Copy(self.pool, q.at[p.right, 2:4], s.at[0, 2:4], p.to_x(p.right), s.at[0, 2:4]),
            Copy(self.pool, q.at[p.left, 0:2], s.at[1, 0:2], p.to_x(p.left), s.at[1, 0:2]),
        ]

    def relay(self):
        p, q, s = self.place, self.parts, self.sums
        self.half_left.arrived()
        for z in (0, 1):
            q[p.right, z] = (
                q[p.right, z].astype(jnp.float32) + self.halves[0, z].astype(jnp.float32)
            ).astype(jnp.bfloat16)
        self.direct.append(
            Copy(self.pool, q.at[p.right, 0:2], s.at[0, 0:2], p.to_x(p.right), s.at[0, 0:2])
        )
        self.half_right.arrived()
        for z in (0, 1):
            q[p.left, z + 2] = (
                q[p.left, z + 2].astype(jnp.float32) + self.halves[1, z].astype(jnp.float32)
            ).astype(jnp.bfloat16)
        self.direct.append(
            Copy(self.pool, q.at[p.left, 2:4], s.at[1, 2:4], p.to_x(p.left), s.at[1, 2:4])
        )

    def z_start(self):
        p = self.place
        for copy in self.direct:
            copy.arrived()

        def total(z):
            return (
                self.parts[p.x, z].astype(jnp.float32)
                + self.sums[0, z].astype(jnp.float32)
                + self.sums[1, z].astype(jnp.float32)
            )

        self.z_copies = []
        for step in (1, 2, 3):
            z = (p.z + step) % 4
            self.z_out[step - 1] = total(z).astype(jnp.bfloat16)
            self.z_copies.append(
                Copy(
                    self.pool, self.z_out.at[step - 1], self.z_in.at[step - 1], p.to_z(z),
                    self.z_in.at[step - 1],
                )
            )
        self.own = total(p.z)

    def finish(self):
        for copy in self.z_copies:
            copy.arrived()
        return (
            self.own
            + self.z_in[0].astype(jnp.float32)
            + self.z_in[1].astype(jnp.float32)
            + self.z_in[2].astype(jnp.float32)
        )


class ColReduce:
    def __init__(self, place, pool, parts, halves, sums, low_out, low_in, own, result):
        self.place, self.pool, self.parts = place, pool, parts
        self.halves, self.sums, self.low_out, self.low_in = halves, sums, low_out, low_in
        self.own, self.result = own, result

    def start(self):
        p, q, s, h = self.place, self.parts, self.sums, self.halves
        right, left = p.to_y(p.y_right), p.to_y(p.y_left)
        self.half_left = Copy(self.pool, q.at[0, p.y_far], h.at[0], right, h.at[0])
        self.half_right = Copy(self.pool, q.at[1, p.y_far], h.at[1], left, h.at[1])
        self.direct = [
            Copy(self.pool, q.at[1, p.y_right], s.at[0, 1], right, s.at[0, 1]),
            Copy(self.pool, q.at[0, p.y_left], s.at[1, 0], left, s.at[1, 0]),
        ]

    def relay(self):
        p, q, s = self.place, self.parts, self.sums
        self.half_left.arrived()
        q[0, p.y_right] = (
            q[0, p.y_right].astype(jnp.float32) + self.halves[0].astype(jnp.float32)
        ).astype(jnp.bfloat16)
        self.direct.append(
            Copy(self.pool, q.at[0, p.y_right], s.at[0, 0], p.to_y(p.y_right), s.at[0, 0])
        )
        self.half_right.arrived()
        q[1, p.y_left] = (
            q[1, p.y_left].astype(jnp.float32) + self.halves[1].astype(jnp.float32)
        ).astype(jnp.bfloat16)
        self.direct.append(
            Copy(self.pool, q.at[1, p.y_left], s.at[1, 1], p.to_y(p.y_left), s.at[1, 1])
        )

    def low_start(self):
        p = self.place
        for copy in self.direct:
            copy.arrived()

        def total(low):
            return (
                self.parts[low, p.y].astype(jnp.float32)
                + self.sums[0, low].astype(jnp.float32)
                + self.sums[1, low].astype(jnp.float32)
            )

        self.low_out[...] = total(1 - p.low).astype(jnp.bfloat16)
        self.low_copy = Copy(self.pool, self.low_out, self.low_in, p.to_low(), self.low_in)
        self.own[...] = total(p.low)

    def at(self, low, y):
        return self.result.at[low, y // 2, self.x, y % 2]

    def finish(self, x):
        p, self.x = self.place, x
        self.low_copy.arrived()
        self.result[p.low, p.y // 2, x, p.y % 2] = (
            self.own[...] + self.low_in[...].astype(jnp.float32)
        ).astype(jnp.bfloat16)
        block = self.at(p.low, p.y)
        self.back = Copy(self.pool, block, block, p.to_low(), self.at(1 - p.low, p.y))

    def column(self, y):
        return self.result.at[:, y // 2, self.x, y % 2]

    def y_start(self):
        p = self.place
        self.back.arrived()
        own = self.column(p.y)
        self.from_left = Copy(self.pool, own, own, p.to_y(p.y_right), self.column(p.y_left))
        self.from_right = Copy(self.pool, own, own, p.to_y(p.y_left), self.column(p.y_right))

    def forward(self):
        p = self.place
        self.from_left.arrived()
        low = self.at(0, p.y_left)
        self.far_low = Copy(self.pool, low, low, p.to_y(p.y_right), self.at(0, p.y_far))
        self.from_right.arrived()
        high = self.at(1, p.y_right)
        self.far_high = Copy(self.pool, high, high, p.to_y(p.y_left), self.at(1, p.y_far))

    def wait_far(self):
        self.far_low.arrived()
        self.far_high.arrived()


def scatter_kernel(
    upstream, weight, kv_own, grad_ref, kv_all, other_up, other_weight, parts, halves, sums,
    z_out, z_in, send, recv,
):
    p, pool = Place(), Pool(send, recv)
    chunks = parts.shape[0]
    width = parts.shape[-1]
    greet(p.row_peers())
    other = 1 - p.core
    weight_copy = Copy(pool, weight, other_weight, p.sibling(), other_weight)
    order = (p.far, p.right, p.left, p.x)
    up_copies = [
        Copy(pool, upstream.at[:, x, other], other_up.at[:, x], p.sibling(), other_up.at[:, x])
        for x in order
    ]
    gather = RowGather(p, pool, kv_all)
    gather.z_start(kv_own)
    kv_all[p.z, p.x, p.core] = kv_own[...]
    scatters = [
        RowScatter(p, pool, parts.at[j], halves.at[j], sums.at[j], z_out.at[j], z_in.at[j])
        for j in range(chunks)
    ]

    def multiply(chunk, x):
        cols = pl.ds(chunk * width, width)
        for z in range(4):
            parts[chunk, x, z] = (
                lax.dot_general(
                    upstream[z, x, p.core], weight[cols, :], NT,
                    preferred_element_type=jnp.float32,
                )
                + lax.dot_general(
                    other_up[z, x], other_weight[cols, :], NT,
                    preferred_element_type=jnp.float32,
                )
            ).astype(jnp.bfloat16)

    weight_copy.arrived()
    for j in range(chunks):
        for index, x in enumerate(order):
            if j == 0:
                up_copies[index].arrived()
            multiply(j, x)
            if index == 0:
                scatters[j].far_start()
            if index == 2:
                scatters[j].near_start()
        if j == 0:
            gather.x_start()
    scatters[0].relay()
    gather.forward()
    scatters[1].relay()
    scatters[2].relay()
    scatters[0].z_start()
    gather.far_core()
    scatters[1].z_start()
    scatters[2].z_start()
    for j in range(chunks):
        grad_ref[:, pl.ds(j * width, width)] = scatters[j].finish().astype(jnp.bfloat16)
    for name in ("own", "left", "right", "far"):
        gather.wait_core(name)
    pool.drain()


def scatter_and_gather(upstream, weight, kv_own):
    tok_rows = kv_own.shape[0]
    features = upstream.shape[1]
    heads = weight.shape[0]
    chunks, width = 3, heads // 3
    vmem = pl.BlockSpec(memory_space=pltpu.VMEM)
    bf16 = jnp.bfloat16
    copies = 1 + 4 + 11 + 9 * chunks
    grad, kv_all = pl.pallas_call(
        scatter_kernel,
        out_shape=(
            jax.ShapeDtypeStruct((tok_rows, heads), bf16),
            jax.ShapeDtypeStruct((4, 4, 2, *kv_own.shape), bf16),
        ),
        in_specs=[vmem] * 3,
        out_specs=[vmem] * 2,
        scratch_shapes=[
            pltpu.VMEM((4, 4, tok_rows, features), bf16),
            pltpu.VMEM(weight.shape, bf16),
            pltpu.VMEM((chunks, 4, 4, tok_rows, width), bf16),
            pltpu.VMEM((chunks, 2, 2, tok_rows, width), bf16),
            pltpu.VMEM((chunks, 2, 4, tok_rows, width), bf16),
            pltpu.VMEM((chunks, 3, tok_rows, width), bf16),
            pltpu.VMEM((chunks, 3, tok_rows, width), bf16),
            pltpu.SemaphoreType.DMA((copies,)),
            pltpu.SemaphoreType.DMA((copies,)),
        ],
        compiler_params=pltpu.CompilerParams(
            collective_id=1, has_side_effects=True, vmem_limit_bytes=48 * 2**20
        ),
        name="grad_scatter",
    )(upstream.reshape(4, 4, 2, tok_rows, features), weight, kv_own)
    return grad, kv_all.reshape(-1, kv_own.shape[1])


def attention_kernel(
    stored_ref, kv_ref, grad_ref, attn_ref, dquery_ref, dkv_ref, score_ref, k_t, v_t, total_ref
):
    tok_rows = stored_ref.shape[0]
    tile = KEY_TILE
    first_token = lax.axis_index("row") * tok_rows
    tiles = (first_token + tok_rows + tile - 1) // tile
    pair_cols = 2 * tok_rows
    base2 = HEAD_SIZE ** (-0.5) * LOG2E

    def rows_of(index):
        return pl.ds(pl.multiple_of(index * tile, tile), tile)

    def prepare(index, carry):
        rows = rows_of(index)
        k_t[:, rows] = kv_ref[rows, :HEAD_SIZE].T
        v_t[:, rows] = kv_ref[rows, HEAD_SIZE:].T
        total_ref[rows, :] = jnp.zeros((tile, 2 * HEAD_SIZE), jnp.float32)
        return carry

    lax.fori_loop(0, kv_ref.shape[0] // tile, prepare, 0)

    def two_heads(ref, pair):
        start = pl.multiple_of(pair * 2 * HEAD_SIZE, 2 * HEAD_SIZE)
        both = ref[:, pl.ds(start, 2 * HEAD_SIZE)]
        return jnp.concatenate([both[:, :HEAD_SIZE], both[:, HEAD_SIZE:]], axis=0)

    def put_heads(ref, pair, stacked):
        start = pl.multiple_of(pair * 2 * HEAD_SIZE, 2 * HEAD_SIZE)
        ref[:, pl.ds(start, 2 * HEAD_SIZE)] = jnp.concatenate(
            [stacked[:tok_rows], stacked[tok_rows:]], axis=1
        )

    def one_pair(pair, carry):
        query = two_heads(stored_ref, pair)
        grad = two_heads(grad_ref, pair)
        query_t = query.T
        grad_t = grad.T

        def scores(index):
            return jnp.dot(
                kv_ref[rows_of(index), :HEAD_SIZE], query_t, preferred_element_type=jnp.float32
            )

        def fold(highest, block):
            return jnp.maximum(highest, jnp.max(block.reshape(tile // 8, 8, pair_cols), axis=0))

        def pass_scores(index, highest):
            block = scores(index)
            score_ref[rows_of(index), :] = block
            return fold(highest, block)

        highest = lax.fori_loop(
            0, tiles - 1, pass_scores, jnp.full((8, pair_cols), -3e38, jnp.float32)
        )
        last = tiles - 1
        key_pos = last * tile + lax.broadcasted_iota(jnp.int32, (tile, pair_cols), 0)
        token_pos = first_token + lax.broadcasted_iota(jnp.int32, (tile, pair_cols), 1) % tok_rows
        block = jnp.where(key_pos <= token_pos, scores(last), -1e30)
        score_ref[rows_of(last), :] = block
        highest = jnp.max(fold(highest, block), axis=0, keepdims=True) * base2

        def pass_exp(index, carry):
            total_exp, out_t = carry
            rows = rows_of(index)
            expon = jnp.exp2(score_ref[rows, :] * base2 - highest)
            score_ref[rows, :] = expon
            total_exp = total_exp + jnp.sum(expon.reshape(tile // 8, 8, pair_cols), axis=0)
            out_t = out_t + jnp.dot(
                v_t[:, rows], expon.astype(jnp.bfloat16), preferred_element_type=jnp.float32
            )
            return (total_exp, out_t)

        total_exp, out_t = lax.fori_loop(
            0,
            tiles,
            pass_exp,
            (
                jnp.zeros((8, pair_cols), jnp.float32),
                jnp.zeros((HEAD_SIZE, pair_cols), jnp.float32),
            ),
        )
        inverse = 1.0 / jnp.sum(total_exp, axis=0, keepdims=True)
        out_t = out_t * inverse
        delta = jnp.sum(out_t * grad_t.astype(jnp.float32), axis=0, keepdims=True)
        put_heads(attn_ref, pair, out_t.T.astype(jnp.bfloat16))

        def pass_grad(index, dquery_t):
            rows = rows_of(index)
            probs = score_ref[rows, :] * inverse
            dprob = jnp.dot(kv_ref[rows, HEAD_SIZE:], grad_t, preferred_element_type=jnp.float32)
            dscore = (probs * (dprob - delta)).astype(jnp.bfloat16)
            total_ref[rows, :HEAD_SIZE] += jnp.dot(
                dscore, query, preferred_element_type=jnp.float32
            )
            total_ref[rows, HEAD_SIZE:] += jnp.dot(
                probs.astype(jnp.bfloat16), grad, preferred_element_type=jnp.float32
            )
            return dquery_t + jnp.dot(k_t[:, rows], dscore, preferred_element_type=jnp.float32)

        dquery_t = lax.fori_loop(
            0, tiles, pass_grad, jnp.zeros((HEAD_SIZE, pair_cols), jnp.float32)
        )
        put_heads(
            dquery_ref, pair, (dquery_t * HEAD_SIZE ** (-0.5)).T.astype(jnp.bfloat16)
        )
        return carry

    lax.fori_loop(0, QUERIES_PER_KV // 2, one_pair, 0)

    def finish(index, carry):
        rows = rows_of(index)
        dkv_ref[rows, :HEAD_SIZE] = (total_ref[rows, :HEAD_SIZE] * HEAD_SIZE ** (-0.5)).astype(
            dkv_ref.dtype
        )
        dkv_ref[rows, HEAD_SIZE:] = total_ref[rows, HEAD_SIZE:].astype(dkv_ref.dtype)
        return carry

    lax.fori_loop(0, kv_ref.shape[0] // tile, finish, 0)


def attention(stored, kv, grad_attn, dkv_type):
    tok_rows, all_tokens = stored.shape[0], kv.shape[0]
    heads = QUERIES_PER_KV * HEAD_SIZE
    vmem = pl.BlockSpec(memory_space=pltpu.VMEM)
    pair_cols = 2 * tok_rows
    return pl.pallas_call(
        attention_kernel,
        out_shape=(
            jax.ShapeDtypeStruct((tok_rows, heads), jnp.bfloat16),
            jax.ShapeDtypeStruct((tok_rows, heads), jnp.bfloat16),
            jax.ShapeDtypeStruct((all_tokens, 2 * HEAD_SIZE), dkv_type),
        ),
        in_specs=[vmem] * 3,
        out_specs=[vmem] * 3,
        scratch_shapes=[
            pltpu.VMEM((all_tokens, pair_cols), jnp.float32),
            pltpu.VMEM((HEAD_SIZE, all_tokens), jnp.bfloat16),
            pltpu.VMEM((HEAD_SIZE, all_tokens), jnp.bfloat16),
            pltpu.VMEM((all_tokens, 2 * HEAD_SIZE), jnp.float32),
        ],
        compiler_params=pltpu.CompilerParams(vmem_limit_bytes=48 * 2**20),
        name="attention",
    )(stored, kv, grad_attn)
def finish_kernel(
    attn, dquery, dkv_part, upstream, activations, weight, grad_act, grad_joined, grad_output,
    attn_all, dquery_all, dkv_all, other_dkv, parts, halves, sums, z_out, z_in, up_t, act_t,
    y_parts, y_halves, y_sums, low_out, low_in, y_own, joined_sum, output_sum, send, recv,
):
    p, pool = Place(), Pool(send, recv)
    f32, bf16 = jnp.float32, jnp.bfloat16
    width = dkv_all.shape[-1]
    pairs = dquery_all.shape[0]
    greet(p.row_peers() + p.col_peers())
    other = 1 - p.core
    order = (p.far, p.right, p.left, p.x)
    dkv_copies = [
        Copy(pool, dkv_part.at[:, x, other], other_dkv.at[:, x], p.sibling(), other_dkv.at[:, x])
        for x in order
    ]

    def gathers(local_ref, buffer):
        made = []
        for j in range(pairs):
            buffer[j, p.z, p.x, p.core] = local_ref[:, j * width : (j + 1) * width]
            made.append(RowGather(p, pool, buffer.at[j]))
        return made

    def z_starts(made, buffer):
        for j in range(pairs):
            made[j].z_start(buffer.at[j, p.z, p.x, p.core])

    g_query = gathers(dquery, dquery_all)
    z_starts(g_query, dquery_all)
    g_attn = gathers(attn, attn_all)
    g_dkv = RowGather(p, pool, dkv_all)
    scatter = RowScatter(p, pool, parts, halves, sums, z_out, z_in)

    def transposed(source, target):
        def step(index, carry):
            target[index] = source[index].T
            return carry

        lax.fori_loop(0, source.shape[0], step, 0)

    def add_dkv(index):
        x = order[index]
        dkv_copies[index].arrived()
        for z in range(4):
            parts[x, z] = (
                dkv_part[z, x, p.core].astype(f32) + other_dkv[z, x].astype(f32)
            ).astype(bf16)

    add_dkv(0)
    scatter.far_start()
    add_dkv(1)
    add_dkv(2)
    scatter.near_start()
    add_dkv(3)
    g_query[0].x_start()
    scatter.relay()
    transposed(activations, act_t)
    scatter.z_start()
    g_query[1].x_start()
    g_query[2].x_start()
    dkv_all[p.z, p.x, p.core] = scatter.finish().astype(bf16)
    g_dkv.z_start(dkv_all.at[p.z, p.x, p.core])
    z_starts(g_attn, attn_all)
    transposed(upstream, up_t)
    g_query[0].forward()
    g_dkv.x_start()
    g_query[1].forward()
    g_query[2].forward()
    g_attn[0].x_start()
    g_dkv.forward()
    g_attn[1].x_start()
    g_attn[2].x_start()

    reduces = [
        ColReduce(
            p, pool, y_parts.at[i], y_halves.at[i], y_sums.at[i], low_out.at[i], low_in.at[i],
            y_own.at[i], grad_act,
        )
        for i in range(4)
    ]
    xs = (p.x, p.left, p.right, p.far)
    names = ("own", "left", "right", "far")

    def both(ref, z, x):
        return ref[z, x].reshape(2 * ref.shape[3], width)

    def head_grads(i):
        x = xs[i]
        operands = [dquery_all.at[j] for j in range(pairs)] + [dkv_all]
        for gather in [*g_query, g_dkv]:
            gather.wait_core(names[i])
        for z in range(4):
            total = 0.0
            for j, ref in enumerate(operands):
                total = total + lax.dot_general(
                    both(ref, z, x), weight[:, j * width : (j + 1) * width], NT,
                    preferred_element_type=f32,
                )
            total = total.astype(bf16)
            rows = total.shape[0] // 2
            y_parts[i, z // 2, (z % 2) * 2] = total[:rows]
            y_parts[i, z // 2, (z % 2) * 2 + 1] = total[rows:]
        reduces[i].start()

    def joined(i):
        x = xs[i]
        operands = [dquery_all.at[j] for j in range(pairs)] + [dkv_all]
        for j, ref in enumerate(operands):
            cols = slice(j * width, (j + 1) * width)
            total = joined_sum[:, cols] if i else 0.0
            for z in range(4):
                total = total + jnp.dot(
                    act_t[z * 4 + x], both(ref, z, x), preferred_element_type=f32
                )
            if i < 3:
                joined_sum[:, cols] = total
            else:
                grad_joined[:, cols] = total.astype(bf16)

    def output(i):
        x = xs[i]
        for j in range(pairs):
            g_attn[j].wait_core(names[i])
            cols = slice(j * width, (j + 1) * width)
            total = output_sum[:, cols] if i else 0.0
            for z in range(4):
                total = total + jnp.dot(
                    up_t[z * 4 + x], both(attn_all.at[j], z, x), preferred_element_type=f32
                )
            if i < 3:
                output_sum[:, cols] = total
            else:
                grad_output[cols, :] = total.T.astype(bf16)

    head_grads(0)
    joined(0)
    g_query[0].far_core()
    head_grads(1)
    reduces[0].relay()
    joined(1)
    g_query[1].far_core()
    head_grads(2)
    reduces[0].low_start()
    reduces[1].relay()
    g_query[2].far_core()
    g_dkv.far_core()
    joined(2)
    g_attn[0].forward()
    reduces[0].finish(xs[0])
    reduces[1].low_start()
    reduces[2].relay()
    head_grads(3)
    g_attn[1].forward()
    reduces[0].y_start()
    reduces[1].finish(xs[1])
    reduces[2].low_start()
    reduces[3].relay()
    joined(3)
    g_attn[2].forward()
    reduces[0].forward()
    reduces[1].y_start()
    reduces[2].finish(xs[2])
    reduces[3].low_start()
    output(0)
    reduces[1].forward()
    reduces[2].y_start()
    reduces[3].finish(xs[3])
    g_attn[0].far_core()
    g_attn[1].far_core()
    reduces[2].forward()
    reduces[3].y_start()
    output(1)
    g_attn[2].far_core()
    reduces[3].forward()
    output(2)
    output(3)
    for reduce in reduces:
        reduce.wait_far()
    pool.drain()


def finish(attn, dquery, dkv_part, upstream, activations, weight):
    tok_rows, heads = attn.shape
    all_tokens, width = dkv_part.shape
    features = upstream.shape[1]
    pairs = heads // width
    bf16, f32 = jnp.bfloat16, jnp.float32
    vmem = pl.BlockSpec(memory_space=pltpu.VMEM)
    copies = 4 + 11 * (2 * pairs + 1) + 9 + 4 * 12
    block = (tok_rows, width)
    cells = all_tokens // (2 * tok_rows)
    grad_act, grad_joined, grad_output = pl.pallas_call(
        finish_kernel,
        out_shape=(
            jax.ShapeDtypeStruct((2, 2, 4, 2, tok_rows, features), bf16),
            jax.ShapeDtypeStruct((features, weight.shape[1]), bf16),
            jax.ShapeDtypeStruct((heads, features), bf16),
        ),
        in_specs=[vmem] * 6,
        out_specs=[vmem] * 3,
        scratch_shapes=[
            pltpu.VMEM((pairs, 4, 4, 2, *block), bf16),
            pltpu.VMEM((pairs, 4, 4, 2, *block), bf16),
            pltpu.VMEM((4, 4, 2, *block), bf16),
            pltpu.VMEM((4, 4, *block), bf16),
            pltpu.VMEM((4, 4, *block), bf16),
            pltpu.VMEM((2, 2, *block), bf16),
            pltpu.VMEM((2, 4, *block), bf16),
            pltpu.VMEM((3, *block), bf16),
            pltpu.VMEM((3, *block), bf16),
            pltpu.VMEM((cells, features, 2 * tok_rows), bf16),
            pltpu.VMEM((cells, features, 2 * tok_rows), bf16),
            pltpu.VMEM((4, 2, 4, tok_rows, features), bf16),
            pltpu.VMEM((4, 2, tok_rows, features), bf16),
            pltpu.VMEM((4, 2, 2, tok_rows, features), bf16),
            pltpu.VMEM((4, tok_rows, features), bf16),
            pltpu.VMEM((4, tok_rows, features), bf16),
            pltpu.VMEM((4, tok_rows, features), f32),
            pltpu.VMEM((features, weight.shape[1]), f32),
            pltpu.VMEM((features, heads), f32),
            pltpu.SemaphoreType.DMA((copies,)),
            pltpu.SemaphoreType.DMA((copies,)),
        ],
        compiler_params=pltpu.CompilerParams(
            collective_id=2, has_side_effects=True, vmem_limit_bytes=56 * 2**20
        ),
        name="gather_and_multiply",
    )(
        attn,
        dquery,
        dkv_part.reshape(4, 4, 2, tok_rows, width),
        upstream.reshape(cells, 2 * tok_rows, features),
        activations.reshape(cells, 2 * tok_rows, features),
        weight,
    )
    return grad_act.reshape(all_tokens, features), grad_joined, grad_output


def local(activations, stored, joined_weight, output_weight, upstream):
    heads = QUERIES_PER_KV * HEAD_SIZE
    grad_attn, kv = scatter_and_gather(upstream, output_weight, stored[:, heads:])
    attn_local, dquery_local, dkv_part = attention(stored, kv, grad_attn, jnp.bfloat16)
    return finish(attn_local, dquery_local, dkv_part, upstream, activations, joined_weight)


def solution(mesh):
    return jax.shard_map(
        local,
        mesh=mesh,
        in_specs=(
            P(None, "row"),
            P("row", "col"),
            P("row", "col"),
            P("col", "row"),
            P(None, "row"),
        ),
        out_specs=(P(None, "row"), P("row", "col"), P("col", "row")),
        check_vma=False,
    )
```
